32 devices in a mesh: span: 2 (over x), pitch: 4 (over y, core), chord: 4 (over z).
Axes of the slice: x: 2, y: 2, z: 4, core: 2. Of those that a mesh axis runs over, the one named last changes fastest.
Arguments:
- adjoint_start: float32 [3, 32, 128, 512], P(None, 'span', 'pitch', 'chord'), may hold values from -6 to 6
- sensitivity_source: float32 [3, 32, 128, 512], P(None, 'span', 'pitch', 'chord'), may hold values from -6 to 6
- stiffness_class: int32 [32, 128, 512], P('span', 'pitch', 'chord'), may hold values from 0 to 7
- stiffness_table: float32 [8], replicated, may hold values from 0.25 to 4
- wall_cell: int32 [32768], P(('span', 'pitch', 'chord')), may hold values from 0 to 65535
- patch_owner: int32 [32768, 1], P(('span', 'pitch', 'chord')), may hold values from 0 to 511; in each aligned block of 1024 rows (0 to 1023, 1024 to 2047, ...) at most 4 rows name the same one
- wall_normal: float32 [3, 32768], P(None, ('span', 'pitch', 'chord')), may hold values from -1 to 1
- mode_shape: float32 [8, 32768], P(None, ('span', 'pitch', 'chord')), may hold values from -6 to 6
Outputs:
- adjoint: float32 [3, 32, 128, 512], P(None, 'span', 'pitch', 'chord')
- patch_grad: float32 [8, 4096], P(None, ('span', 'pitch', 'chord'))
The draws below stay inside these ranges and needn't reach their ends.
Inputs may be any that keep to these rules, and one draw needn't show every extreme that they name: `patch_owner`: within the rows of one device, no patch is named by more than 4 rows, a bound that some block reaches.
All inputs are finite; a program needn't handle non-finite values.
Results may differ from the reference program's by a relative error of at most 0.00018.
Values sent between devices are 32-bit elements; how exact they have to be, the bound alone decides.
A program may use at most 64 MiB of HBM per device.

```python
import math
import jax
import jax.numpy as jnp
import numpy as np

CX = 16
CY = 32
CZ = 128
PATCH_DEV = 128
CAP = 4
MODES = 8
NCLASS = 8
SWEEPS = 3
NX = 32
NY = 128
NZ = 512
WALL = 1024
WALL_TOTAL = 32768
PATCHES = 4096
N_PITCH = 4
N_CHORD = 4


def with_ends(values, stream_key, smallest, largest):
    longest = values.shape.index(max(values.shape))
    spots = []
    for shift in (0, 1):
        where = [jax.random.randint(jax.random.fold_in(stream_key, axis), (), 0, length) for axis, length in enumerate(values.shape)]
        where[longest] = (where[longest] + shift) % values.shape[longest]
        spots.append(tuple(where))
    return values.at[spots[0]].set(smallest).at[spots[1]].set(largest)


def steps_of(stream_key, shape, cuts, low, high):
    level, own = 1.0, jax.random.fold_in(stream_key, 6)
    for dim, shards_of in cuts:
        steps = jnp.exp(jax.random.uniform(jax.random.fold_in(own, dim), (shards_of,), jnp.float32, low / len(cuts), high / len(cuts)))
        level = level * jnp.repeat(steps, shape[dim] // shards_of).reshape([-1 if axis == dim else 1 for axis in range(len(shape))])
    return level


def deal_out(key, own, number, rows, number_of, top, bound, slope):
    ranking = jax.random.permutation(key, number_of)
    crowded, usual = shares(number_of, rows * top, bound, slope, True), shares(number_of, rows * top, bound, slope, False)
    places = jnp.arange(number_of)

    def named(sizes, rotation):
        used = int((sizes > 0).sum())
        fixed = max(1, used // 4)
        moved = fixed + (places - fixed + rotation * (used - fixed)) % max(1, number_of - fixed)
        return jnp.zeros((number_of,), jnp.int32).at[ranking[jnp.where(places < fixed, places, moved)]].set(jnp.asarray(sizes, jnp.int32))

    sizes = jnp.where(number % 4 == 0, named(crowded, number // 4), named(usual, number - number // 4 - 1))
    mixed = jax.random.permutation(jax.random.fold_in(own, 3), number_of)
    giver, receiver = mixed[0:number_of // 2 * 2:2], mixed[1:number_of // 2 * 2:2]
    slack = jnp.minimum(sizes[giver] - 1, bound - sizes[receiver]) // 2
    slack = jnp.where((giver == ranking[0]) | (receiver == ranking[0]) | (sizes[receiver] == 0), 0, jnp.maximum(slack, 0))
    moved = jax.random.randint(jax.random.fold_in(own, 4), (number_of // 2,), 0, 1 << 20) % (slack + 1)
    sizes = sizes.at[giver].add(-moved).at[receiver].add(moved)
    items = jnp.searchsorted(jnp.cumsum(sizes), jnp.arange(rows * top), side="right").astype(jnp.int32)
    listing = items.reshape(top, rows).T
    listing = listing[jax.random.permutation(jax.random.fold_in(own, 1), rows)]
    rotation = jax.random.randint(jax.random.fold_in(own, 2), (rows, 1), 0, top)
    return jnp.take_along_axis(listing, (jnp.arange(top)[None, :] + rotation) % top, axis=1)


def shares(count, total, reach, skew, full):
    weights = [(1 << 20) // math.isqrt(rank ** skew) + 1 for rank in range(1, count + 1)]
    largest = reach if full else min(reach, max(-(-total // count), total * weights[0] // sum(weights)))
    least = 1 if total - largest >= count - 1 else 0
    counts, rest = [largest] + [least] * (count - 1), total - largest - least * (count - 1)
    while rest > 0:
        free = [i for i in range(1, count) if counts[i] < largest] or [i for i in range(1, count) if counts[i] < reach]
        pool, budget = sum([weights[i] for i in free]), rest
        for i in free:
            extra = min(reach - counts[i], max(1, budget * weights[i] // pool), rest)
            counts[i] = counts[i] + extra
            rest = rest - extra
    return np.array(counts)


def gaussian(key, shape, spread, limit, cuts=(), kind=jnp.bfloat16):
    entries = spread * jax.random.normal(key, shape, jnp.float32)
    if cuts:
        entries = entries * steps_of(key, shape, cuts, -0.22, 0.18)
    return jnp.clip(entries, -limit, limit).astype(kind)


def setup_inputs(seed: int = 0) -> dict:
    key_list = jax.random.split(jax.random.key(seed), 9)
    adjoint_start = gaussian(key_list[0], (3, NX, NY, NZ), 1.0, 6.0, ((1, 2), (2, 4), (3, 4)), jnp.float32)
    sensitivity_source = gaussian(key_list[1], (3, NX, NY, NZ), 1.0, 6.0, ((1, 2), (2, 4), (3, 4)), jnp.float32)
    stiffness_class = with_ends(jax.random.randint(key_list[2], (NX, NY, NZ), 0, NCLASS), jax.random.fold_in(key_list[2], 1), 0, NCLASS - 1).astype(jnp.int32)
    stiffness_table = jnp.clip(jnp.exp(jax.random.uniform(key_list[3], (NCLASS,), jnp.float32, math.log(0.25), math.log(4.0))), 0.25, 4.0)
    wall_cell = with_ends(jax.random.randint(key_list[4], (WALL_TOTAL,), 0, CX * CY * CZ), jax.random.fold_in(key_list[4], 1), 0, (CX * CY * CZ) - 1).astype(jnp.int32)
    patch_owner_keys = jax.random.split(jax.random.fold_in(key_list[5], 1), WALL_TOTAL // WALL)
    patch_owner_turns = jax.random.permutation(jax.random.fold_in(key_list[5], 3), WALL_TOTAL // WALL)
    patch_owner = jax.vmap(lambda own, number: deal_out(jax.random.fold_in(key_list[5], 2), own, number, WALL, PATCH_DEV * N_CHORD, 1, CAP, 2))(patch_owner_keys, patch_owner_turns).reshape((WALL_TOTAL, 1))
    wall_normal = jnp.clip(jax.random.uniform(key_list[6], (3, WALL_TOTAL), jnp.float32, -1.0, 1.0) * steps_of(key_list[6], (3, WALL_TOTAL), ((1, 32),), -0.4, 0.0), -1.0, 1.0)
    mode_shape = gaussian(key_list[7], (MODES, WALL_TOTAL), 1.0, 6.0, ((1, 32),), jnp.float32)
    return {"adjoint_start": adjoint_start, "sensitivity_source": sensitivity_source, "stiffness_class": stiffness_class, "stiffness_table": stiffness_table, "wall_cell": wall_cell, "patch_owner": patch_owner, "wall_normal": wall_normal, "mode_shape": mode_shape}


MASS_SHIFT = 0.5
RELAXATION = 0.8
DIAGONAL_SUM = 10.5
LAME_WEIGHTS = ((3.0, 1.0, 1.0), (1.0, 3.0, 1.0), (1.0, 1.0, 3.0))


def stiffness_from(classes, table):
    result = jnp.zeros(classes.shape, jnp.float32)
    for number in range(table.shape[0]):
        result = result + jnp.where(classes == number, table[number], 0.0)
    return result


def operator_image(padded):
    center = padded[:, 1:-1, 1:-1, 1:-1]
    along_span = 2.0 * center - padded[:, 2:, 1:-1, 1:-1] - padded[:, :-2, 1:-1, 1:-1]
    along_pitch = 2.0 * center - padded[:, 1:-1, 2:, 1:-1] - padded[:, 1:-1, :-2, 1:-1]
    along_chord = 2.0 * center - padded[:, 1:-1, 1:-1, 2:] - padded[:, 1:-1, 1:-1, :-2]
    weights = jnp.array(LAME_WEIGHTS, jnp.float32)
    image = MASS_SHIFT * center
    image = image + weights[:, 0][:, None, None, None] * along_span
    image = image + weights[:, 1][:, None, None, None] * along_pitch
    image = image + weights[:, 2][:, None, None, None] * along_chord
    return image


def relax_step(adjoint, source, stiffness, image):
    return adjoint + RELAXATION * (source - image) / (DIAGONAL_SUM * stiffness)


def reference(adjoint_start, sensitivity_source, stiffness_class, stiffness_table, wall_cell, patch_owner, wall_normal, mode_shape):
    stiffness = stiffness_from(stiffness_class, stiffness_table)
    adjoint = adjoint_start
    for sweep_index in range(SWEEPS):
        product = stiffness[None] * adjoint
        padded = jnp.pad(product, ((0, 0), (1, 1), (1, 1), (1, 1)))
        adjoint = relax_step(adjoint, sensitivity_source, stiffness, operator_image(padded))
    row_index = jnp.arange(WALL_TOTAL, dtype=jnp.int32)
    device = row_index // WALL
    span_pos = device // (N_PITCH * N_CHORD)
    pitch_pos = (device // N_CHORD) % N_PITCH
    chord_pos = device % N_CHORD
    first_coord = span_pos * CX + wall_cell // (CY * CZ)
    second_coord = pitch_pos * CY + (wall_cell // CZ) % CY
    third_coord = chord_pos * CZ + wall_cell % CZ
    traction_field = stiffness[None] * adjoint
    traction = traction_field[:, first_coord, second_coord, third_coord]
    normal_part = jnp.sum(wall_normal * traction, axis=0)
    contribution = mode_shape * normal_part[None]
    patch_index = ((span_pos * N_PITCH + pitch_pos) * N_CHORD) * PATCH_DEV + patch_owner[:, 0]
    patch_grad = jnp.zeros((MODES, PATCHES), jnp.float32).at[:, patch_index].add(contribution)
    return adjoint, patch_grad
```

```python
import functools

import jax
import jax.numpy as jnp
from jax import lax
from jax.experimental import pallas as pl
from jax.experimental.pallas import tpu as pltpu
from jax.sharding import PartitionSpec as P

MESH = pl.DeviceIdType.MESH
AXES = ("span", "pitch", "chord")
PATCH_DEV = 128
MODES = 8
SWEEPS = 3
RELAXATION = 0.8
DIAGONAL_SUM = 10.5
STEP = RELAXATION / DIAGONAL_SUM
KEEP = 1.0 - RELAXATION
OFF_WEIGHT = 1.0
OWN_WEIGHT = 3.0
F32 = jnp.float32
BF16 = jnp.bfloat16


def weight(component, dim):
    return OWN_WEIGHT if component == dim else OFF_WEIGHT


def split(value):
    high = value.astype(BF16)
    low = (value - high.astype(F32)).astype(BF16)
    return high, low


def kernel(
    sizes,
    start_hbm,
    source_hbm,
    class_hbm,
    table,
    cell_hbm,
    owner_hbm,
    normal_hbm,
    mode_hbm,
    adjoint_hbm,
    patch_out,
    start,
    source,
    classes,
    cell,
    owner,
    normal,
    mode,
    stiff,
    inverse,
    prod,
    halo_x,
    halo_y,
    halo_z,
    face_y,
    face_z,
    result,
    pieces,
    depth_hot,
    patch_hot,
    group_send,
    group_recv,
    in_sem,
    small_sem,
    out_sem,
    send_sem,
    recv_sem,
    group_send_sem,
    group_recv_sem,
):
    _, cx, cy, cz = start.shape
    rows = cell.shape[1]
    chord_count = sizes[2]
    me = [lax.axis_index(name) for name in AXES]
    has = [(me[d] > 0, me[d] < sizes[d] - 1) for d in range(3)]
    partner = [(me[d] - 1, me[d] + 1) for d in range(3)]
    peers = [lax.rem(me[2] + i, chord_count) for i in range(chord_count)]

    barrier = pltpu.get_barrier_semaphore()
    greeted = jnp.int32(chord_count - 1)
    for d in range(2):
        for side in range(2):
            greeted = greeted + has[d][side].astype(jnp.int32)

            @pl.when(has[d][side])
            def _(d=d, side=side):
                pl.semaphore_signal(
                    barrier, inc=1, device_id={AXES[d]: partner[d][side]}, device_id_type=MESH
                )

    for i in range(1, chord_count):
        pl.semaphore_signal(barrier, inc=1, device_id={"chord": peers[i]}, device_id_type=MESH)

    load_class = pltpu.make_async_copy(class_hbm, classes, in_sem.at[0])
    load_start = [
        pltpu.make_async_copy(start_hbm.at[c], start.at[c], in_sem.at[1 + c]) for c in range(3)
    ]
    load_source = [
        pltpu.make_async_copy(source_hbm.at[c], source.at[c], in_sem.at[4 + c]) for c in range(3)
    ]
    load_small = [
        pltpu.make_async_copy(cell_hbm, cell, small_sem.at[0]),
        pltpu.make_async_copy(owner_hbm, owner, small_sem.at[1]),
        pltpu.make_async_copy(normal_hbm, normal, small_sem.at[2]),
        pltpu.make_async_copy(mode_hbm, mode, small_sem.at[3]),
    ]
    for copy in [load_class] + load_start + load_source + load_small:
        copy.start()

    for d, halo in ((0, halo_x), (1, halo_y), (2, halo_z)):
        for side in range(2):

            @pl.when(jnp.logical_not(has[d][side]))
            def _(halo=halo, side=side):
                for k in range(SWEEPS):
                    for c in range(3):
                        halo[k, c, side] = jnp.zeros(halo.shape[3:], F32)

    lane = lax.broadcasted_iota(jnp.int32, (cy, cz), 1)
    row = lax.broadcasted_iota(jnp.int32, (cy, cz), 0)
    row8 = lax.broadcasted_iota(jnp.int32, (8, cz), 0)
    lane8 = lax.broadcasted_iota(jnp.int32, (8, cz), 1)
    pair = lane // 2
    edge = (lane == 0) | (lane == cz - 1)
    blocks = cy // 8
    order = [0, cx - 1] + list(range(1, cx - 1))

    def transfer(k, c, d, side):
        other = 1 - side
        if d == 0:
            src, dst = prod.at[k, c, (cx - 1) * side], halo_x.at[k, c, other]
        elif d == 1:
            src, dst = face_y.at[k, c, side], halo_y.at[k, c, other]
        else:
            src, dst = face_z.at[k, c], halo_z.at[k, c, other]
        return pltpu.make_async_remote_copy(
            src_ref=src,
            dst_ref=dst,
            send_sem=send_sem.at[k, c, d, side],
            recv_sem=recv_sem.at[k, c, d, other],
            device_id={AXES[d]: partner[d][side]},
            device_id_type=MESH,
        )

    def send(k, c, d):
        for side in range(2):

            @pl.when(has[d][side])
            def _(side=side):
                transfer(k, c, d, side).start()

    def receive(k, c):
        for d in (2, 1, 0):
            for side in range(2):

                @pl.when(has[d][side])
                def _(d=d, side=side):
                    transfer(k, c, d, 1 - side).wait_recv()

    def emit(k, c, value_at, before_send=None):
        packed = jnp.zeros((cy, cz), F32)
        for place, x in enumerate(order):
            value = value_at(x)
            prod[k, c, x] = value
            face_y[k, c, 0, x : x + 1, :] = value[0:1]
            face_y[k, c, 1, x : x + 1, :] = value[cy - 1 : cy]
            packed = jnp.where(pair == x, pltpu.roll(value, 2 * x + 1, 1), packed)
            if place == 1:
                if before_send is not None:
                    before_send()
                send(k, c, 0)
        tile = packed[0:8]
        stride = cz // blocks
        for b in range(1, blocks):
            tile = tile + pltpu.roll(packed[8 * b : 8 * b + 8], stride * b, 1)
        face_z[k, c] = tile
        send(k, c, 2)
        send(k, c, 1)

    def interior(k, c):
        for x in range(cx):
            here = prod[k, c, x]
            if x == 0:
                span_sum = prod[k, c, 1]
            elif x == cx - 1:
                span_sum = prod[k, c, cx - 2]
            else:
                span_sum = prod[k, c, x - 1] + prod[k, c, x + 1]
            pitch_sum = jnp.where(row == 0, 0.0, pltpu.roll(here, 1, 0)) + jnp.where(
                row == cy - 1, 0.0, pltpu.roll(here, cy - 1, 0)
            )
            chord_sum = jnp.where(lane == 0, 0.0, pltpu.roll(here, 1, 1)) + jnp.where(
                lane == cz - 1, 0.0, pltpu.roll(here, cz - 1, 1)
            )
            sums = (span_sum, pitch_sum, chord_sum)
            total = span_sum + pitch_sum + chord_sum + (OWN_WEIGHT - OFF_WEIGHT) * sums[c]
            prod[k + 1, c, x] = KEEP * here + STEP * (source[c, x] + total)

    def finished(k, c):
        left, right = halo_z[k, c, 0], halo_z[k, c, 1]
        joined = jnp.where(lane8 % 2 == 0, left, pltpu.roll(right, cz - 2, 1))
        joined = (STEP * weight(c, 2)) * joined
        stride = cz // blocks
        spread = jnp.concatenate(
            [joined] + [pltpu.roll(joined, cz - stride * b, 1) for b in range(1, blocks)], axis=0
        )

        def value_at(x):
            value = prod[k + 1, c, x]
            turned = spread if x == 0 else pltpu.roll(spread, cz - 2 * x, 1)
            value = value + jnp.where(edge, turned, 0.0)
            if x == 0:
                value = value + (STEP * weight(c, 0)) * halo_x[k, c, 0]
            if x == cx - 1:
                value = value + (STEP * weight(c, 0)) * halo_x[k, c, 1]
            low = (STEP * weight(c, 1)) * halo_y[k, c, 0, x : x + 1, :]
            high = (STEP * weight(c, 1)) * halo_y[k, c, 1, x : x + 1, :]
            first = value[0:8] + jnp.where(row8 == 0, low, 0.0)
            last = value[cy - 8 : cy] + jnp.where(row8 == 7, high, 0.0)
            return jnp.concatenate([first, value[8 : cy - 8], last], axis=0)

        return value_at

    load_class.wait()

    def first_value(c):
        def value_at(x):
            if c == 0:
                number = classes[x]
                level = jnp.full((cy, cz), table[0], F32)
                for i in range(1, table.shape[0]):
                    level = jnp.where(number == i, table[i], level)
                stiff[x] = level
            else:
                level = stiff[x]
            return level * start[c, x]

        return value_at

    for c in range(3):
        load_start[c].wait()
        meet = (lambda: pl.semaphore_wait(barrier, greeted)) if c == 0 else None
        emit(0, c, first_value(c), meet)
    for c in range(3):
        load_source[c].wait()
        interior(0, c)

    for copy in load_small:
        copy.wait()
    depth_of = cell[...] % cz
    plane_of = cell[...] // cz
    span_of = plane_of // cy
    pitch_of = plane_of % cy

    def build_tables():
        depth = lax.broadcasted_iota(jnp.int32, (cz, rows), 0)
        hot = jnp.where(depth == depth_of, 1.0, 0.0).astype(BF16)
        depth_hot[0:cz, :] = hot
        depth_hot[cz : 2 * cz, :] = hot
        for x in range(cx):
            inverse[x] = 1.0 / stiff[x]

    def build_patches():
        patch = lax.broadcasted_iota(jnp.int32, (PATCH_DEV, rows), 0)
        for j in range(chord_count):
            hot = jnp.where(patch == owner[...] - PATCH_DEV * j, 1.0, 0.0).astype(BF16)
            patch_hot[PATCH_DEV * j : PATCH_DEV * (j + 1), :] = hot

    build_tables()
    for k in range(SWEEPS - 1):
        for c in range(3):
            receive(k, c)
            emit(k + 1, c, finished(k, c))
            interior(k + 1, c)
        if k == 0:
            build_patches()

    width = 256
    parts = [jnp.zeros((1, width), F32) for _ in range(rows // width)]
    store = []
    k = SWEEPS - 1
    for c in range(3):
        receive(k, c)
        value_at = finished(k, c)
        for x in range(cx):
            value = value_at(x)
            result[c, x] = value * inverse[x]
            high, low = split(value)
            pieces[c, cy * x : cy * (x + 1), 0:cz] = high
            pieces[c, cy * x : cy * (x + 1), cz : 2 * cz] = low
        copy = pltpu.make_async_copy(result.at[c], adjoint_hbm.at[c], out_sem.at[c])
        copy.start()
        store.append(copy)
        for n in range(rows // width):
            cut = slice(width * n, width * (n + 1))
            picked = jnp.dot(
                pieces[c], depth_hot[:, cut], preferred_element_type=F32
            )
            chosen = picked[0:cy]
            for x in range(1, cx):
                chosen = jnp.where(
                    span_of[:, cut] == x, picked[cy * x : cy * (x + 1)], chosen
                )
            place = lax.broadcasted_iota(jnp.int32, (cy, width), 0)
            chosen = jnp.where(place == pitch_of[:, cut], chosen, 0.0)
            traction = jnp.sum(chosen, axis=0, keepdims=True)
            parts[n] = parts[n] + normal[c : c + 1, cut] * traction

    contribution = jnp.concatenate(
        [mode[:, width * n : width * (n + 1)] * parts[n] for n in range(rows // width)], axis=1
    )
    high, low = split(contribution)
    both = jnp.concatenate([high, low], axis=0)
    grouped = lax.dot_general(
        both, patch_hot[...], (((1,), (1,)), ((), ())), preferred_element_type=F32
    )
    grouped = grouped[0:MODES] + grouped[MODES : 2 * MODES]
    for j in range(chord_count):
        group_send[j] = grouped[:, PATCH_DEV * j : PATCH_DEV * (j + 1)]

    exchange = []
    for i in range(1, chord_count):
        copy = pltpu.make_async_remote_copy(
            src_ref=group_send.at[peers[i]],
            dst_ref=group_recv.at[i],
            send_sem=group_send_sem.at[i],
            recv_sem=group_recv_sem.at[i],
            device_id={"chord": peers[i]},
            device_id_type=MESH,
        )
        copy.start()
        exchange.append(copy)

    for d in range(3):
        for side in range(2):

            @pl.when(has[d][side])
            def _(d=d, side=side):
                for k in range(SWEEPS):
                    for c in range(3):
                        transfer(k, c, d, side).wait_send()

    total = group_send[me[2]]
    for i, copy in enumerate(exchange):
        copy.wait()
        total = total + group_recv[i + 1]
    patch_out[...] = total
    for copy in store:
        copy.wait()


def body(sizes, start, source, classes, table, cell, owner, normal, mode):
    _, cx, cy, cz = start.shape
    rows = cell.shape[0]
    chord_count = sizes[2]
    hbm = pl.BlockSpec(memory_space=pl.ANY)
    vmem = pltpu.VMEM
    dma = pltpu.SemaphoreType.DMA
    return pl.pallas_call(
        functools.partial(kernel, sizes),
        out_shape=(
            jax.ShapeDtypeStruct(start.shape, F32),
            jax.ShapeDtypeStruct((MODES, PATCH_DEV), F32),
        ),
        in_specs=[hbm, hbm, hbm, pl.BlockSpec(memory_space=pltpu.SMEM), hbm, hbm, hbm, hbm],
        out_specs=(hbm, pl.BlockSpec(memory_space=pltpu.VMEM)),
        scratch_shapes=[
            vmem(start.shape, F32),
            vmem(start.shape, F32),
            vmem((cx, cy, cz), jnp.int32),
            vmem((1, rows), jnp.int32),
            vmem((1, rows), jnp.int32),
            vmem((3, rows), F32),
            vmem((MODES, rows), F32),
            vmem((cx, cy, cz), F32),
            vmem((cx, cy, cz), F32),
            vmem((SWEEPS + 1, 3, cx, cy, cz), F32),
            vmem((SWEEPS, 3, 2, cy, cz), F32),
            vmem((SWEEPS, 3, 2, cx, cz), F32),
            vmem((SWEEPS, 3, 2, 8, cz), F32),
            vmem((SWEEPS, 3, 2, cx, cz), F32),
            vmem((SWEEPS, 3, 8, cz), F32),
            vmem(start.shape, F32),
            vmem((3, cx * cy, 2 * cz), BF16),
            vmem((2 * cz, rows), BF16),
            vmem((chord_count * PATCH_DEV, rows), BF16),
            vmem((chord_count, MODES, PATCH_DEV), F32),
            vmem((chord_count, MODES, PATCH_DEV), F32),
            dma((7,)),
            dma((4,)),
            dma((3,)),
            dma((SWEEPS, 3, 3, 2)),
            dma((SWEEPS, 3, 3, 2)),
            dma((chord_count,)),
            dma((chord_count,)),
        ],
        compiler_params=pltpu.CompilerParams(
            collective_id=0, has_side_effects=True, vmem_limit_bytes=56 * 1024 * 1024
        ),
        cost_estimate=pl.CostEstimate(
            flops=2 * 1024 * 1024 * 1024, bytes_accessed=3 * 1024 * 1024, transcendentals=0
        ),
    )(
        start,
        source,
        classes,
        table,
        cell.reshape(1, rows),
        owner.reshape(1, rows),
        normal,
        mode,
    )


def solution(mesh):
    sizes = tuple(mesh.shape[name] for name in AXES)
    field = P(None, "span", "pitch", "chord")
    listing = P(None, AXES)
    in_specs = (field, field, P(*AXES), P(), P(AXES), P(AXES, None), listing, listing)
    return jax.shard_map(
        functools.partial(body, sizes),
        mesh=mesh,
        in_specs=in_specs,
        out_specs=(field, listing),
        check_vma=False,
    )
```

```python
import functools

import jax
import jax.numpy as jnp
from jax import lax
from jax.experimental import pallas as pl
from jax.experimental.pallas import tpu as pltpu
from jax.sharding import PartitionSpec as P

MESH = pl.DeviceIdType.MESH
AXES = ("span", "pitch", "chord")
PATCH_DEV = 128
MODES = 8
SWEEPS = 3
RELAXATION = 0.8
DIAGONAL_SUM = 10.5
STEP = RELAXATION / DIAGONAL_SUM
KEEP = 1.0 - RELAXATION
OFF_WEIGHT = 1.0
OWN_WEIGHT = 3.0
F32 = jnp.float32
BF16 = jnp.bfloat16


def step_weight(component, dim):
    return jnp.where(component == dim, F32(STEP * OWN_WEIGHT), F32(STEP * OFF_WEIGHT))


def split(value):
    high = value.astype(BF16)
    low = (value - high.astype(F32)).astype(BF16)
    return high, low


def kernel(
    sizes,
    start_hbm,
    source_hbm,
    class_hbm,
    table,
    cell_hbm,
    owner_hbm,
    normal_hbm,
    mode_hbm,
    adjoint_out,
    patch_out,
    start,
    source,
    classes,
    cell,
    owner,
    normal,
    mode,
    stiff,
    inverse,
    prod,
    halo_x,
    halo_y,
    halo_z,
    face_y,
    face_z,
    traction,
    pieces,
    depth_hot,
    patch_hot,
    group_send,
    group_recv,
    in_sem,
    small_sem,
    send_sem,
    recv_sem,
    group_send_sem,
    group_recv_sem,
):
    _, cx, cy, cz = start.shape
    rows = cell.shape[1]
    chord_count = sizes[2]
    me = [lax.axis_index(name) for name in AXES]
    has = [(me[d] > 0, me[d] < sizes[d] - 1) for d in range(3)]
    partner = [(me[d] - 1, me[d] + 1) for d in range(3)]
    peers = [lax.rem(me[2] + i, chord_count) for i in range(chord_count)]

    barrier = pltpu.get_barrier_semaphore()
    greeted = jnp.int32(chord_count - 1)
    for d in range(2):
        for side in range(2):
            greeted = greeted + has[d][side].astype(jnp.int32)

            @pl.when(has[d][side])
            def _(d=d, side=side):
                pl.semaphore_signal(
                    barrier, inc=1, device_id={AXES[d]: partner[d][side]}, device_id_type=MESH
                )

    for i in range(1, chord_count):
        pl.semaphore_signal(barrier, inc=1, device_id={"chord": peers[i]}, device_id_type=MESH)

    load_class = pltpu.make_async_copy(class_hbm, classes, in_sem.at[0])
    load_start = [
        pltpu.make_async_copy(start_hbm.at[c], start.at[c], in_sem.at[1 + c]) for c in range(3)
    ]
    load_source = [
        pltpu.make_async_copy(source_hbm.at[c], source.at[c], in_sem.at[4 + c]) for c in range(3)
    ]
    load_small = [
        pltpu.make_async_copy(cell_hbm, cell, small_sem.at[0]),
        pltpu.make_async_copy(owner_hbm, owner, small_sem.at[1]),
        pltpu.make_async_copy(normal_hbm, normal, small_sem.at[2]),
        pltpu.make_async_copy(mode_hbm, mode, small_sem.at[3]),
    ]
    for copy in [load_class] + load_start + load_source + load_small:
        copy.start()

    for d, halo in ((0, halo_x), (1, halo_y), (2, halo_z)):
        for side in range(2):

            @pl.when(jnp.logical_not(has[d][side]))
            def _(halo=halo, side=side):
                for k in range(SWEEPS):
                    for c in range(3):
                        halo[k, c, side] = jnp.zeros(halo.shape[3:], F32)

    lane = lax.broadcasted_iota(jnp.int32, (cy, cz), 1)
    row = lax.broadcasted_iota(jnp.int32, (cy, cz), 0)
    row8 = lax.broadcasted_iota(jnp.int32, (8, cz), 0)
    lane8 = lax.broadcasted_iota(jnp.int32, (8, cz), 1)
    pair = lane // 2
    edge = (lane == 0) | (lane == cz - 1)
    blocks = cy // 8
    order = [0, cx - 1] + list(range(1, cx - 1))

    def transfer(k, c, d, side):
        other = 1 - side
        if d == 0:
            src, dst = prod.at[k, c, (cx - 1) * side], halo_x.at[k, c, other]
        elif d == 1:
            src, dst = face_y.at[k, c, side], halo_y.at[k, c, other]
        else:
            src, dst = face_z.at[k, c], halo_z.at[k, c, other]
        return pltpu.make_async_remote_copy(
            src_ref=src,
            dst_ref=dst,
            send_sem=send_sem.at[k, c, d, side],
            recv_sem=recv_sem.at[k, c, d, other],
            device_id={AXES[d]: partner[d][side]},
            device_id_type=MESH,
        )

    def send(k, c, d):
        for side in range(2):

            @pl.when(has[d][side])
            def _(side=side):
                transfer(k, c, d, side).start()

    def receive(k, c):
        for d in (2, 1, 0):
            for side in range(2):

                @pl.when(has[d][side])
                def _(d=d, side=side):
                    transfer(k, c, d, 1 - side).wait_recv()

    def emit(k, c, value_at):
        packed = jnp.zeros((cy, cz), F32)
        for place, x in enumerate(order):
            value = value_at(x)
            prod[k, c, x] = value
            face_y[k, c, 0, x : x + 1, :] = value[0:1]
            face_y[k, c, 1, x : x + 1, :] = value[cy - 1 : cy]
            packed = jnp.where(pair == x, pltpu.roll(value, 2 * x + 1, 1), packed)
            if place == 1:
                send(k, c, 0)
        tile = packed[0:8]
        stride = cz // blocks
        for b in range(1, blocks):
            tile = tile + pltpu.roll(packed[8 * b : 8 * b + 8], stride * b, 1)
        face_z[k, c] = tile
        send(k, c, 2)
        send(k, c, 1)

    def interior(k, c):
        weights = [step_weight(c, d) for d in range(3)]
        for x in range(cx):
            here = prod[k, c, x]
            if x == 0:
                span_sum = prod[k, c, 1]
            elif x == cx - 1:
                span_sum = prod[k, c, cx - 2]
            else:
                span_sum = prod[k, c, x - 1] + prod[k, c, x + 1]
            pitch_sum = jnp.where(row == 0, 0.0, pltpu.roll(here, 1, 0)) + jnp.where(
                row == cy - 1, 0.0, pltpu.roll(here, cy - 1, 0)
            )
            chord_sum = jnp.where(lane == 0, 0.0, pltpu.roll(here, 1, 1)) + jnp.where(
                lane == cz - 1, 0.0, pltpu.roll(here, cz - 1, 1)
            )
            around = weights[0] * span_sum + weights[1] * pitch_sum + weights[2] * chord_sum
            prod[k + 1, c, x] = KEEP * here + STEP * source[c, x] + around

    def finished(k, c):
        left, right = halo_z[k, c, 0], halo_z[k, c, 1]
        joined = jnp.where(lane8 % 2 == 0, left, pltpu.roll(right, cz - 2, 1))
        weights = [step_weight(c, d) for d in range(3)]
        joined = weights[2] * joined
        stride = cz // blocks
        spread = jnp.concatenate(
            [joined] + [pltpu.roll(joined, cz - stride * b, 1) for b in range(1, blocks)], axis=0
        )

        def value_at(x):
            value = prod[k + 1, c, x]
            turned = spread if x == 0 else pltpu.roll(spread, cz - 2 * x, 1)
            value = value + jnp.where(edge, turned, 0.0)
            if x == 0:
                value = value + weights[0] * halo_x[k, c, 0]
            if x == cx - 1:
                value = value + weights[0] * halo_x[k, c, 1]
            low = weights[1] * halo_y[k, c, 0, x : x + 1, :]
            high = weights[1] * halo_y[k, c, 1, x : x + 1, :]
            first = value[0:8] + jnp.where(row8 == 0, low, 0.0)
            last = value[cy - 8 : cy] + jnp.where(row8 == 7, high, 0.0)
            return jnp.concatenate([first, value[8 : cy - 8], last], axis=0)

        return value_at

    load_class.wait()

    for x in range(cx):
        number = classes[x]
        level = jnp.full((cy, cz), table[0], F32)
        for i in range(1, table.shape[0]):
            level = jnp.where(number == i, table[i], level)
        stiff[x] = level
    pl.semaphore_wait(barrier, greeted)

    def first(c, _):
        pltpu.make_async_copy(start_hbm.at[c], start.at[c], in_sem.at[1 + c]).wait()
        emit(0, c, lambda x: stiff[x] * start[c, x])
        return 0

    def inner(c, _):
        pltpu.make_async_copy(source_hbm.at[c], source.at[c], in_sem.at[4 + c]).wait()
        interior(0, c)
        return 0

    lax.fori_loop(0, 3, first, 0)
    lax.fori_loop(0, 3, inner, 0)

    for copy in load_small:
        copy.wait()
    depth_of = cell[...] % cz
    plane_of = cell[...] // cz
    span_of = plane_of // cy
    pitch_of = plane_of % cy

    def build_tables():
        depth = lax.broadcasted_iota(jnp.int32, (cz, rows), 0)
        hot = jnp.where(depth == depth_of, 1.0, 0.0).astype(BF16)
        depth_hot[0:cz, :] = hot
        depth_hot[cz : 2 * cz, :] = hot
        for x in range(cx):
            inverse[x] = 1.0 / stiff[x]

    def build_patches():
        patch = lax.broadcasted_iota(jnp.int32, (PATCH_DEV, rows), 0)
        for j in range(chord_count):
            hot = jnp.where(patch == owner[...] - PATCH_DEV * j, 1.0, 0.0).astype(BF16)
            patch_hot[PATCH_DEV * j : PATCH_DEV * (j + 1), :] = hot

    build_tables()
    build_patches()

    def sweep(number, _):
        k, c = number // 3, number % 3
        receive(k, c)
        emit(k + 1, c, finished(k, c))
        interior(k + 1, c)
        return 0

    lax.fori_loop(0, 3 * (SWEEPS - 1), sweep, 0)

    width = 256

    def last(c, _):
        receive(SWEEPS - 1, c)
        value_at = finished(SWEEPS - 1, c)
        for x in range(cx):
            value = value_at(x)
            adjoint_out[c, x] = value * inverse[x]
            high, low = split(value)
            pieces[c, cy * x : cy * (x + 1), 0:cz] = high
            pieces[c, cy * x : cy * (x + 1), cz : 2 * cz] = low
        for n in range(rows // width):
            cut = slice(width * n, width * (n + 1))
            picked = jnp.dot(pieces[c], depth_hot[:, cut], preferred_element_type=F32)
            chosen = picked[0:cy]
            for x in range(1, cx):
                chosen = jnp.where(
                    span_of[:, cut] == x, picked[cy * x : cy * (x + 1)], chosen
                )
            place = lax.broadcasted_iota(jnp.int32, (cy, width), 0)
            chosen = jnp.where(place == pitch_of[:, cut], chosen, 0.0)
            traction[c, :, cut] = jnp.sum(chosen, axis=0, keepdims=True)
        return 0

    lax.fori_loop(0, 3, last, 0)
    normal_part = sum(normal[c : c + 1, :] * traction[c] for c in range(3))

    contribution = mode[...] * normal_part
    high, low = split(contribution)
    both = jnp.concatenate([high, low], axis=0)
    grouped = lax.dot_general(
        both, patch_hot[...], (((1,), (1,)), ((), ())), preferred_element_type=F32
    )
    grouped = grouped[0:MODES] + grouped[MODES : 2 * MODES]
    for j in range(chord_count):
        group_send[j] = grouped[:, PATCH_DEV * j : PATCH_DEV * (j + 1)]

    exchange = []
    for i in range(1, chord_count):
        copy = pltpu.make_async_remote_copy(
            src_ref=group_send.at[peers[i]],
            dst_ref=group_recv.at[i],
            send_sem=group_send_sem.at[i],
            recv_sem=group_recv_sem.at[i],
            device_id={"chord": peers[i]},
            device_id_type=MESH,
        )
        copy.start()
        exchange.append(copy)

    for d in range(3):
        for side in range(2):

            @pl.when(has[d][side])
            def _(d=d, side=side):
                for k in range(SWEEPS):
                    for c in range(3):
                        transfer(k, c, d, side).wait_send()

    total = group_send[me[2]]
    for i, copy in enumerate(exchange):
        copy.wait()
        total = total + group_recv[i + 1]
    patch_out[...] = total


def write(adjoint, patches, adjoint_hbm, patch_hbm, sem):
    copies = [
        pltpu.make_async_copy(adjoint, adjoint_hbm, sem.at[0]),
        pltpu.make_async_copy(patches, patch_hbm, sem.at[1]),
    ]
    for copy in copies:
        copy.start()
    for copy in copies:
        copy.wait()


def body(sizes, start, source, classes, table, cell, owner, normal, mode):
    _, cx, cy, cz = start.shape
    rows = cell.shape[0]
    chord_count = sizes[2]
    hbm = pl.BlockSpec(memory_space=pl.ANY)
    main = pl.BlockSpec(memory_space=pltpu.HBM)
    vmem = pltpu.VMEM
    dma = pltpu.SemaphoreType.DMA
    adjoint, patches = pl.pallas_call(
        functools.partial(kernel, sizes),
        out_shape=(vmem(start.shape, F32), vmem((MODES, PATCH_DEV), F32)),
        in_specs=[main, main, main, pl.BlockSpec(memory_space=pltpu.SMEM), main, main, main, main],
        out_specs=(pl.BlockSpec(memory_space=vmem), pl.BlockSpec(memory_space=vmem)),
        scratch_shapes=[
            vmem(start.shape, F32),
            vmem(start.shape, F32),
            vmem((cx, cy, cz), jnp.int32),
            vmem((1, rows), jnp.int32),
            vmem((1, rows), jnp.int32),
            vmem((3, rows), F32),
            vmem((MODES, rows), F32),
            vmem((cx, cy, cz), F32),
            vmem((cx, cy, cz), F32),
            vmem((SWEEPS + 1, 3, cx, cy, cz), F32),
            vmem((SWEEPS, 3, 2, cy, cz), F32),
            vmem((SWEEPS, 3, 2, cx, cz), F32),
            vmem((SWEEPS, 3, 2, 8, cz), F32),
            vmem((SWEEPS, 3, 2, cx, cz), F32),
            vmem((SWEEPS, 3, 8, cz), F32),
            vmem((3, 1, rows), F32),
            vmem((3, cx * cy, 2 * cz), BF16),
            vmem((2 * cz, rows), BF16),
            vmem((chord_count * PATCH_DEV, rows), BF16),
            vmem((chord_count, MODES, PATCH_DEV), F32),
            vmem((chord_count, MODES, PATCH_DEV), F32),
            dma((7,)),
            dma((4,)),
            dma((SWEEPS, 3, 3, 2)),
            dma((SWEEPS, 3, 3, 2)),
            dma((chord_count,)),
            dma((chord_count,)),
        ],
        compiler_params=pltpu.CompilerParams(
            collective_id=0, has_side_effects=True, vmem_limit_bytes=63 * 1024 * 1024
        ),
        cost_estimate=pl.CostEstimate(
            flops=2 * 1024 * 1024 * 1024, bytes_accessed=3 * 1024 * 1024, transcendentals=0
        ),
    )(
        start,
        source,
        classes,
        table,
        cell.reshape(1, rows),
        owner.reshape(1, rows),
        normal,
        mode,
    )
    return pl.pallas_call(
        write,
        out_shape=(
            jax.ShapeDtypeStruct(adjoint.shape, F32),
            jax.ShapeDtypeStruct(patches.shape, F32),
        ),
        in_specs=[hbm, hbm],
        out_specs=(hbm, hbm),
        scratch_shapes=[dma((2,))],
    )(adjoint, patches)


def solution(mesh):
    sizes = tuple(mesh.shape[name] for name in AXES)
    field = P(None, "span", "pitch", "chord")
    listing = P(None, AXES)
    in_specs = (field, field, P(*AXES), P(), P(AXES), P(AXES, None), listing, listing)
    return jax.shard_map(
        functools.partial(body, sizes),
        mesh=mesh,
        in_specs=in_specs,
        out_specs=(field, listing),
        check_vma=False,
    )
```

```python
import functools

import jax
import jax.numpy as jnp
from jax import lax
from jax.experimental import pallas as pl
from jax.experimental.pallas import tpu as pltpu
from jax.sharding import PartitionSpec as P

MESH = pl.DeviceIdType.MESH
AXES = ("span", "pitch", "chord")
PATCH_DEV = 128
MODES = 8
SWEEPS = 3
RELAXATION = 0.8
DIAGONAL_SUM = 10.5
STEP = RELAXATION / DIAGONAL_SUM
KEEP = 1.0 - RELAXATION
OFF_WEIGHT = 1.0
OWN_WEIGHT = 3.0
F32 = jnp.float32
BF16 = jnp.bfloat16


def step_weight(component, dim):
    return jnp.where(component == dim, F32(STEP * OWN_WEIGHT), F32(STEP * OFF_WEIGHT))


def split(value):
    high = value.astype(BF16)
    low = (value - high.astype(F32)).astype(BF16)
    return high, low


def kernel(
    sizes,
    start_hbm,
    source_hbm,
    class_hbm,
    table,
    cell_hbm,
    owner_hbm,
    normal_hbm,
    mode_hbm,
    adjoint_out,
    patch_out,
    start,
    source,
    classes,
    cell,
    owner,
    normal,
    mode,
    stiff,
    inverse,
    prod,
    halo_x,
    halo_y,
    halo_z,
    face_y,
    face_z,
    traction,
    pieces,
    depth_hot,
    patch_hot,
    group_send,
    group_recv,
    in_sem,
    small_sem,
    send_sem,
    recv_sem,
    group_send_sem,
    group_recv_sem,
):
    _, cx, cy, cz = start.shape
    rows = cell.shape[1]
    chord_count = sizes[2]
    me = [lax.axis_index(name) for name in AXES]
    has = [(me[d] > 0, me[d] < sizes[d] - 1) for d in range(3)]
    partner = [(me[d] - 1, me[d] + 1) for d in range(3)]
    peers = [lax.rem(me[2] + i, chord_count) for i in range(chord_count)]

    barrier = pltpu.get_barrier_semaphore()
    greeted = jnp.int32(chord_count - 1)
    for d in range(2):
        for side in range(2):
            greeted = greeted + has[d][side].astype(jnp.int32)

            @pl.when(has[d][side])
            def _(d=d, side=side):
                pl.semaphore_signal(
                    barrier, inc=1, device_id={AXES[d]: partner[d][side]}, device_id_type=MESH
                )

    for i in range(1, chord_count):
        pl.semaphore_signal(barrier, inc=1, device_id={"chord": peers[i]}, device_id_type=MESH)

    load_class = pltpu.make_async_copy(class_hbm, classes, in_sem.at[0])
    load_start = [
        pltpu.make_async_copy(start_hbm.at[c], start.at[c], in_sem.at[1 + c]) for c in range(3)
    ]
    load_source = [
        pltpu.make_async_copy(source_hbm.at[c], source.at[c], in_sem.at[4 + c]) for c in range(3)
    ]
    load_small = [
        pltpu.make_async_copy(cell_hbm, cell, small_sem.at[0]),
        pltpu.make_async_copy(owner_hbm, owner, small_sem.at[1]),
        pltpu.make_async_copy(normal_hbm, normal, small_sem.at[2]),
        pltpu.make_async_copy(mode_hbm, mode, small_sem.at[3]),
    ]
    for copy in [load_class] + load_start + load_source + load_small:
        copy.start()

    for d, halo in ((0, halo_x), (1, halo_y), (2, halo_z)):
        for side in range(2):

            @pl.when(jnp.logical_not(has[d][side]))
            def _(halo=halo, side=side):
                for k in range(SWEEPS):
                    for c in range(3):
                        halo[k, c, side] = jnp.zeros(halo.shape[3:], F32)

    lane = lax.broadcasted_iota(jnp.int32, (cy, cz), 1)
    row = lax.broadcasted_iota(jnp.int32, (cy, cz), 0)
    row8 = lax.broadcasted_iota(jnp.int32, (8, cz), 0)
    lane8 = lax.broadcasted_iota(jnp.int32, (8, cz), 1)
    pair = lane // 2
    edge = (lane == 0) | (lane == cz - 1)
    blocks = cy // 8
    order = [0, cx - 1] + list(range(1, cx - 1))

    def transfer(k, c, d, side):
        other = 1 - side
        if d == 0:
            src, dst = prod.at[k, c, (cx - 1) * side], halo_x.at[k, c, other]
        elif d == 1:
            src, dst = face_y.at[k, c, side], halo_y.at[k, c, other]
        else:
            src, dst = face_z.at[k, c], halo_z.at[k, c, other]
        return pltpu.make_async_remote_copy(
            src_ref=src,
            dst_ref=dst,
            send_sem=send_sem.at[k, c, d, side],
            recv_sem=recv_sem.at[k, c, d, other],
            device_id={AXES[d]: partner[d][side]},
            device_id_type=MESH,
        )

    def send(k, c, d):
        for side in range(2):

            @pl.when(has[d][side])
            def _(side=side):
                transfer(k, c, d, side).start()

    def receive(k, c):
        for d in (2, 1, 0):
            for side in range(2):

                @pl.when(has[d][side])
                def _(d=d, side=side):
                    transfer(k, c, d, 1 - side).wait_recv()

    def emit(k, c, value_at):
        packed = jnp.zeros((cy, cz), F32)
        for place, x in enumerate(order):
            value = value_at(x)
            prod[k, c, x] = value
            face_y[k, c, 0, x : x + 1, :] = value[0:1]
            face_y[k, c, 1, x : x + 1, :] = value[cy - 1 : cy]
            packed = jnp.where(pair == x, pltpu.roll(value, 2 * x + 1, 1), packed)
            if place == 1:
                send(k, c, 0)
        tile = packed[0:8]
        stride = cz // blocks
        for b in range(1, blocks):
            tile = tile + pltpu.roll(packed[8 * b : 8 * b + 8], stride * b, 1)
        face_z[k, c] = tile
        send(k, c, 2)
        send(k, c, 1)

    def interior(k, c):
        weights = [step_weight(c, d) for d in range(3)]
        for x in range(cx):
            here = prod[k, c, x]
            if x == 0:
                span_sum = prod[k, c, 1]
            elif x == cx - 1:
                span_sum = prod[k, c, cx - 2]
            else:
                span_sum = prod[k, c, x - 1] + prod[k, c, x + 1]
            pitch_sum = jnp.where(row == 0, 0.0, pltpu.roll(here, 1, 0)) + jnp.where(
                row == cy - 1, 0.0, pltpu.roll(here, cy - 1, 0)
            )
            chord_sum = jnp.where(lane == 0, 0.0, pltpu.roll(here, 1, 1)) + jnp.where(
                lane == cz - 1, 0.0, pltpu.roll(here, cz - 1, 1)
            )
            around = weights[0] * span_sum + weights[1] * pitch_sum + weights[2] * chord_sum
            prod[k + 1, c, x] = KEEP * here + STEP * source[c, x] + around

    def finished(k, c):
        left, right = halo_z[k, c, 0], halo_z[k, c, 1]
        joined = jnp.where(lane8 % 2 == 0, left, pltpu.roll(right, cz - 2, 1))
        weights = [step_weight(c, d) for d in range(3)]
        joined = weights[2] * joined
        stride = cz // blocks
        spread = jnp.concatenate(
            [joined] + [pltpu.roll(joined, cz - stride * b, 1) for b in range(1, blocks)], axis=0
        )

        def value_at(x):
            value = prod[k + 1, c, x]
            turned = spread if x == 0 else pltpu.roll(spread, cz - 2 * x, 1)
            value = value + jnp.where(edge, turned, 0.0)
            if x == 0:
                value = value + weights[0] * halo_x[k, c, 0]
            if x == cx - 1:
                value = value + weights[0] * halo_x[k, c, 1]
            low = weights[1] * halo_y[k, c, 0, x : x + 1, :]
            high = weights[1] * halo_y[k, c, 1, x : x + 1, :]
            first = value[0:8] + jnp.where(row8 == 0, low, 0.0)
            last = value[cy - 8 : cy] + jnp.where(row8 == 7, high, 0.0)
            return jnp.concatenate([first, value[8 : cy - 8], last], axis=0)

        return value_at

    load_class.wait()

    for x in range(cx):
        number = classes[x]
        level = jnp.full((cy, cz), table[0], F32)
        for i in range(1, table.shape[0]):
            level = jnp.where(number == i, table[i], level)
        stiff[x] = level
    pl.semaphore_wait(barrier, greeted)

    def first(c, _):
        pltpu.make_async_copy(start_hbm.at[c], start.at[c], in_sem.at[1 + c]).wait()
        emit(0, c, lambda x: stiff[x] * start[c, x])
        return 0

    def inner(c, _):
        pltpu.make_async_copy(source_hbm.at[c], source.at[c], in_sem.at[4 + c]).wait()
        interior(0, c)
        return 0

    lax.fori_loop(0, 3, first, 0)
    lax.fori_loop(0, 3, inner, 0)

    for copy in load_small:
        copy.wait()
    depth_of = cell[...] % cz
    plane_of = cell[...] // cz
    span_of = plane_of // cy
    pitch_of = plane_of % cy

    def build_tables():
        depth = lax.broadcasted_iota(jnp.int32, (cz, rows), 0)
        hot = jnp.where(depth == depth_of, 1.0, 0.0).astype(BF16)
        depth_hot[0:cz, :] = hot
        depth_hot[cz : 2 * cz, :] = hot
        for x in range(cx):
            inverse[x] = 1.0 / stiff[x]

    def build_patches():
        patch = lax.broadcasted_iota(jnp.int32, (PATCH_DEV, rows), 0)
        for j in range(chord_count):
            hot = jnp.where(patch == owner[...] - PATCH_DEV * j, 1.0, 0.0).astype(BF16)
            patch_hot[PATCH_DEV * j : PATCH_DEV * (j + 1), :] = hot

    build_tables()
    build_patches()

    def sweep(number, _):
        k, c = number // 3, number % 3
        receive(k, c)
        emit(k + 1, c, finished(k, c))
        interior(k + 1, c)
        return 0

    lax.fori_loop(0, 3 * (SWEEPS - 1), sweep, 0)

    width = 256

    def last(c, _):
        receive(SWEEPS - 1, c)
        value_at = finished(SWEEPS - 1, c)
        for x in range(cx):
            value = value_at(x)
            adjoint_out[c, x] = value * inverse[x]
            high, low = split(value)
            pieces[c, cy * x : cy * (x + 1), 0:cz] = high
            pieces[c, cy * x : cy * (x + 1), cz : 2 * cz] = low
        for n in range(rows // width):
            cut = slice(width * n, width * (n + 1))
            picked = jnp.dot(pieces[c], depth_hot[:, cut], preferred_element_type=F32)
            chosen = picked[0:cy]
            for x in range(1, cx):
                chosen = jnp.where(
                    span_of[:, cut] == x, picked[cy * x : cy * (x + 1)], chosen
                )
            place = lax.broadcasted_iota(jnp.int32, (cy, width), 0)
            chosen = jnp.where(place == pitch_of[:, cut], chosen, 0.0)
            traction[c, :, cut] = jnp.sum(chosen, axis=0, keepdims=True)
        return 0

    lax.fori_loop(0, 3, last, 0)
    normal_part = sum(normal[c : c + 1, :] * traction[c] for c in range(3))

    contribution = mode[...] * normal_part
    high, low = split(contribution)
    both = jnp.concatenate([high, low], axis=0)
    grouped = lax.dot_general(
        both, patch_hot[...], (((1,), (1,)), ((), ())), preferred_element_type=F32
    )
    grouped = grouped[0:MODES] + grouped[MODES : 2 * MODES]
    for j in range(chord_count):
        group_send[j] = grouped[:, PATCH_DEV * j : PATCH_DEV * (j + 1)]

    exchange = []
    for i in range(1, chord_count):
        copy = pltpu.make_async_remote_copy(
            src_ref=group_send.at[peers[i]],
            dst_ref=group_recv.at[i],
            send_sem=group_send_sem.at[i],
            recv_sem=group_recv_sem.at[i],
            device_id={"chord": peers[i]},
            device_id_type=MESH,
        )
        copy.start()
        exchange.append(copy)

    for d in range(3):
        for side in range(2):

            @pl.when(has[d][side])
            def _(d=d, side=side):
                for k in range(SWEEPS):
                    for c in range(3):
                        transfer(k, c, d, side).wait_send()

    total = group_send[me[2]]
    for i, copy in enumerate(exchange):
        copy.wait()
        total = total + group_recv[i + 1]
    patch_out[...] = total


def body(sizes, start, source, classes, table, cell, owner, normal, mode):
    _, cx, cy, cz = start.shape
    rows = cell.shape[0]
    chord_count = sizes[2]
    main = pl.BlockSpec(memory_space=pltpu.HBM)
    vmem = pltpu.VMEM
    dma = pltpu.SemaphoreType.DMA
    return pl.pallas_call(
        functools.partial(kernel, sizes),
        out_shape=(vmem(start.shape, F32), vmem((MODES, PATCH_DEV), F32)),
        in_specs=[main, main, main, pl.BlockSpec(memory_space=pltpu.SMEM), main, main, main, main],
        out_specs=(pl.BlockSpec(memory_space=vmem), pl.BlockSpec(memory_space=vmem)),
        scratch_shapes=[
            vmem(start.shape, F32),
            vmem(start.shape, F32),
            vmem((cx, cy, cz), jnp.int32),
            vmem((1, rows), jnp.int32),
            vmem((1, rows), jnp.int32),
            vmem((3, rows), F32),
            vmem((MODES, rows), F32),
            vmem((cx, cy, cz), F32),
            vmem((cx, cy, cz), F32),
            vmem((SWEEPS + 1, 3, cx, cy, cz), F32),
            vmem((SWEEPS, 3, 2, cy, cz), F32),
            vmem((SWEEPS, 3, 2, cx, cz), F32),
            vmem((SWEEPS, 3, 2, 8, cz), F32),
            vmem((SWEEPS, 3, 2, cx, cz), F32),
            vmem((SWEEPS, 3, 8, cz), F32),
            vmem((3, 1, rows), F32),
            vmem((3, cx * cy, 2 * cz), BF16),
            vmem((2 * cz, rows), BF16),
            vmem((chord_count * PATCH_DEV, rows), BF16),
            vmem((chord_count, MODES, PATCH_DEV), F32),
            vmem((chord_count, MODES, PATCH_DEV), F32),
            dma((7,)),
            dma((4,)),
            dma((SWEEPS, 3, 3, 2)),
            dma((SWEEPS, 3, 3, 2)),
            dma((chord_count,)),
            dma((chord_count,)),
        ],
        compiler_params=pltpu.CompilerParams(
            collective_id=0, has_side_effects=True, vmem_limit_bytes=63 * 1024 * 1024
        ),
        cost_estimate=pl.CostEstimate(
            flops=2 * 1024 * 1024 * 1024, bytes_accessed=3 * 1024 * 1024, transcendentals=0
        ),
    )(
        start,
        source,
        classes,
        table,
        cell.reshape(1, rows),
        owner.reshape(1, rows),
        normal,
        mode,
    )

def solution(mesh):
    sizes = tuple(mesh.shape[name] for name in AXES)
    field = P(None, "span", "pitch", "chord")
    listing = P(None, AXES)
    in_specs = (field, field, P(*AXES), P(), P(AXES), P(AXES, None), listing, listing)
    return jax.shard_map(
        functools.partial(body, sizes),
        mesh=mesh,
        in_specs=in_specs,
        out_specs=(field, listing),
        check_vma=False,
    )
```

```python
import functools

import jax
import jax.numpy as jnp
from jax import lax
from jax.experimental import pallas as pl
from jax.experimental.pallas import tpu as pltpu
from jax.sharding import PartitionSpec as P

MESH = pl.DeviceIdType.MESH
AXES = ("span", "pitch", "chord")
PATCH_DEV = 128
MODES = 8
SWEEPS = 3
RELAXATION = 0.8
DIAGONAL_SUM = 10.5
STEP = RELAXATION / DIAGONAL_SUM
KEEP = 1.0 - RELAXATION
OFF_WEIGHT = 1.0
OWN_WEIGHT = 3.0
F32 = jnp.float32
BF16 = jnp.bfloat16


def step_weight(component, dim):
    return jnp.where(component == dim, F32(STEP * OWN_WEIGHT), F32(STEP * OFF_WEIGHT))


def split(value):
    high = value.astype(BF16)
    low = (value - high.astype(F32)).astype(BF16)
    return high, low


def kernel(
    sizes,
    start_hbm,
    source_hbm,
    class_hbm,
    table,
    cell_hbm,
    owner_hbm,
    normal_hbm,
    mode_hbm,
    adjoint_out,
    patch_out,
    start,
    source,
    classes,
    cell,
    owner,
    normal,
    mode,
    stiff,
    inverse,
    prod,
    halo_x,
    halo_y,
    halo_z,
    face_y,
    face_z,
    traction,
    pieces,
    depth_hot,
    patch_hot,
    group_send,
    group_recv,
    in_sem,
    small_sem,
    send_sem,
    recv_sem,
    group_send_sem,
    group_recv_sem,
):
    _, cx, cy, cz = start.shape
    rows = cell.shape[1]
    chord_count = sizes[2]
    me = [lax.axis_index(name) for name in AXES]
    has = [(me[d] > 0, me[d] < sizes[d] - 1) for d in range(3)]
    partner = [(me[d] - 1, me[d] + 1) for d in range(3)]
    peers = [lax.rem(me[2] + i, chord_count) for i in range(chord_count)]

    barrier = pltpu.get_barrier_semaphore()
    greeted = jnp.int32(chord_count - 1)
    for d in range(2):
        for side in range(2):
            greeted = greeted + has[d][side].astype(jnp.int32)

            @pl.when(has[d][side])
            def _(d=d, side=side):
                pl.semaphore_signal(
                    barrier, inc=1, device_id={AXES[d]: partner[d][side]}, device_id_type=MESH
                )

    for i in range(1, chord_count):
        pl.semaphore_signal(barrier, inc=1, device_id={"chord": peers[i]}, device_id_type=MESH)

    load_class = pltpu.make_async_copy(class_hbm, classes, in_sem.at[0])
    load_start = [
        pltpu.make_async_copy(start_hbm.at[c], start.at[c], in_sem.at[1 + c]) for c in range(3)
    ]
    load_source = [
        pltpu.make_async_copy(source_hbm.at[c], source.at[c], in_sem.at[4 + c]) for c in range(3)
    ]
    load_small = [
        pltpu.make_async_copy(cell_hbm, cell, small_sem.at[0]),
        pltpu.make_async_copy(owner_hbm, owner, small_sem.at[1]),
        pltpu.make_async_copy(normal_hbm, normal, small_sem.at[2]),
        pltpu.make_async_copy(mode_hbm, mode, small_sem.at[3]),
    ]
    for copy in [load_class] + load_start + load_source + load_small:
        copy.start()

    for d, halo in ((0, halo_x), (1, halo_y), (2, halo_z)):
        for side in range(2):

            @pl.when(jnp.logical_not(has[d][side]))
            def _(halo=halo, side=side):
                for k in range(SWEEPS):
                    for c in range(3):
                        halo[k, side, c] = jnp.zeros(halo.shape[3:], F32)

    lane = lax.broadcasted_iota(jnp.int32, (cy, cz), 1)
    row = lax.broadcasted_iota(jnp.int32, (cy, cz), 0)
    row8 = lax.broadcasted_iota(jnp.int32, (8, cz), 0)
    lane8 = lax.broadcasted_iota(jnp.int32, (8, cz), 1)
    pair = lane // 2
    edge = (lane == 0) | (lane == cz - 1)
    blocks = cy // 8
    order = [0, cx - 1] + list(range(1, cx - 1))

    def remote(src, dst, k, slot, d, side):
        other = 1 - side
        return pltpu.make_async_remote_copy(
            src_ref=src,
            dst_ref=dst,
            send_sem=send_sem.at[k, slot, side],
            recv_sem=recv_sem.at[k, slot, other],
            device_id={AXES[d]: me[d] - 1 + 2 * side},
            device_id_type=MESH,
        )

    def span_transfer(k, c, side):
        src = prod.at[k, c, (cx - 1) * side]
        return remote(src, halo_x.at[k, 1 - side, c], k, c, 0, side)

    def pitch_transfer(k, side):
        return remote(face_y.at[k, side], halo_y.at[k, 1 - side], k, 3, 1, side)

    def chord_transfer(k, side):
        return remote(face_z.at[k], halo_z.at[k, 1 - side], k, 4, 2, side)

    def on_span(act):
        if sizes[0] == 2:
            act(1 - me[0])
            return
        for side in range(2):

            @pl.when(has[0][side])
            def _(side=side):
                act(side)

    def on_rest(act):
        for d, move in ((2, chord_transfer), (1, pitch_transfer)):
            for side in range(2):

                @pl.when(has[d][side])
                def _(move=move, side=side):
                    act(move, side)

    def send_span(k, c):
        on_span(lambda side: span_transfer(k, c, side).start())

    def send_rest(k):
        on_rest(lambda move, side: move(k, side).start())

    def receive_span(k, c):
        on_span(lambda side: span_transfer(k, c, 1 - side).wait_recv())

    def receive_rest(k):
        on_rest(lambda move, side: move(k, 1 - side).wait_recv())

    def emit(k, c, value_at):
        packed = jnp.zeros((cy, cz), F32)
        for place, x in enumerate(order):
            value = value_at(x)
            prod[k, c, x] = value
            face_y[k, 0, c, x : x + 1, :] = value[0:1]
            face_y[k, 1, c, x : x + 1, :] = value[cy - 1 : cy]
            packed = jnp.where(pair == x, pltpu.roll(value, 2 * x + 1, 1), packed)
            if place == 1:
                send_span(k, c)
        tile = packed[0:8]
        stride = cz // blocks
        for b in range(1, blocks):
            tile = tile + pltpu.roll(packed[8 * b : 8 * b + 8], stride * b, 1)
        face_z[k, c] = tile

    def interior(k, c):
        weights = [step_weight(c, d) for d in range(3)]
        for x in range(cx):
            here = prod[k, c, x]
            if x == 0:
                span_sum = prod[k, c, 1]
            elif x == cx - 1:
                span_sum = prod[k, c, cx - 2]
            else:
                span_sum = prod[k, c, x - 1] + prod[k, c, x + 1]
            pitch_sum = jnp.where(row == 0, 0.0, pltpu.roll(here, 1, 0)) + jnp.where(
                row == cy - 1, 0.0, pltpu.roll(here, cy - 1, 0)
            )
            chord_sum = jnp.where(lane == 0, 0.0, pltpu.roll(here, 1, 1)) + jnp.where(
                lane == cz - 1, 0.0, pltpu.roll(here, cz - 1, 1)
            )
            around = weights[0] * span_sum + weights[1] * pitch_sum + weights[2] * chord_sum
            prod[k + 1, c, x] = KEEP * here + STEP * source[c, x] + around

    def finished(k, c):
        left, right = halo_z[k, 0, c], halo_z[k, 1, c]
        joined = jnp.where(lane8 % 2 == 0, left, pltpu.roll(right, cz - 2, 1))
        weights = [step_weight(c, d) for d in range(3)]
        joined = weights[2] * joined
        stride = cz // blocks
        spread = jnp.concatenate(
            [joined] + [pltpu.roll(joined, cz - stride * b, 1) for b in range(1, blocks)], axis=0
        )

        def value_at(x):
            value = prod[k + 1, c, x]
            turned = spread if x == 0 else pltpu.roll(spread, cz - 2 * x, 1)
            value = value + jnp.where(edge, turned, 0.0)
            if x == 0:
                value = value + weights[0] * halo_x[k, 0, c]
            if x == cx - 1:
                value = value + weights[0] * halo_x[k, 1, c]
            low = weights[1] * halo_y[k, 0, c, x : x + 1, :]
            high = weights[1] * halo_y[k, 1, c, x : x + 1, :]
            first = value[0:8] + jnp.where(row8 == 0, low, 0.0)
            last = value[cy - 8 : cy] + jnp.where(row8 == 7, high, 0.0)
            return jnp.concatenate([first, value[8 : cy - 8], last], axis=0)

        return value_at

    load_class.wait()

    for x in range(cx):
        number = classes[x]
        level = jnp.full((cy, cz), table[0], F32)
        for i in range(1, table.shape[0]):
            level = jnp.where(number == i, table[i], level)
        stiff[x] = level
    pl.semaphore_wait(barrier, greeted)

    def first(c, _):
        pltpu.make_async_copy(start_hbm.at[c], start.at[c], in_sem.at[1 + c]).wait()
        emit(0, c, lambda x: stiff[x] * start[c, x])
        return 0

    def inner(c, _):
        pltpu.make_async_copy(source_hbm.at[c], source.at[c], in_sem.at[4 + c]).wait()
        interior(0, c)
        return 0

    lax.fori_loop(0, 3, first, 0)
    send_rest(0)
    lax.fori_loop(0, 3, inner, 0)

    for copy in load_small:
        copy.wait()
    depth_of = cell[...] % cz
    plane_of = cell[...] // cz
    span_of = plane_of // cy
    pitch_of = plane_of % cy

    def build_tables():
        depth = lax.broadcasted_iota(jnp.int32, (cz, rows), 0)
        hot = jnp.where(depth == depth_of, 1.0, 0.0).astype(BF16)
        depth_hot[0:cz, :] = hot
        depth_hot[cz : 2 * cz, :] = hot
        for x in range(cx):
            inverse[x] = 1.0 / stiff[x]

    def build_patches():
        patch = lax.broadcasted_iota(jnp.int32, (PATCH_DEV, rows), 0)
        for j in range(chord_count):
            hot = jnp.where(patch == owner[...] - PATCH_DEV * j, 1.0, 0.0).astype(BF16)
            patch_hot[PATCH_DEV * j : PATCH_DEV * (j + 1), :] = hot

    build_tables()
    build_patches()

    def sweep(k, _):
        receive_rest(k)

        def finish(c, _):
            receive_span(k, c)
            emit(k + 1, c, finished(k, c))
            return 0

        def advance(c, _):
            interior(k + 1, c)
            return 0

        lax.fori_loop(0, 3, finish, 0)
        send_rest(k + 1)
        lax.fori_loop(0, 3, advance, 0)
        return 0

    lax.fori_loop(0, SWEEPS - 1, sweep, 0)
    receive_rest(SWEEPS - 1)

    width = 256

    def last(c, _):
        receive_span(SWEEPS - 1, c)
        value_at = finished(SWEEPS - 1, c)
        for x in range(cx):
            value = value_at(x)
            adjoint_out[c, x] = value * inverse[x]
            high, low = split(value)
            pieces[c, cy * x : cy * (x + 1), 0:cz] = high
            pieces[c, cy * x : cy * (x + 1), cz : 2 * cz] = low
        for n in range(rows // width):
            cut = slice(width * n, width * (n + 1))
            picked = jnp.dot(pieces[c], depth_hot[:, cut], preferred_element_type=F32)
            chosen = picked[0:cy]
            for x in range(1, cx):
                chosen = jnp.where(
                    span_of[:, cut] == x, picked[cy * x : cy * (x + 1)], chosen
                )
            place = lax.broadcasted_iota(jnp.int32, (cy, width), 0)
            chosen = jnp.where(place == pitch_of[:, cut], chosen, 0.0)
            traction[c, :, cut] = jnp.sum(chosen, axis=0, keepdims=True)
        return 0

    lax.fori_loop(0, 3, last, 0)
    normal_part = sum(normal[c : c + 1, :] * traction[c] for c in range(3))

    contribution = mode[...] * normal_part
    high, low = split(contribution)
    both = jnp.concatenate([high, low], axis=0)
    grouped = lax.dot_general(
        both, patch_hot[...], (((1,), (1,)), ((), ())), preferred_element_type=F32
    )
    grouped = grouped[0:MODES] + grouped[MODES : 2 * MODES]
    for j in range(chord_count):
        group_send[j] = grouped[:, PATCH_DEV * j : PATCH_DEV * (j + 1)]

    exchange = []
    for i in range(1, chord_count):
        copy = pltpu.make_async_remote_copy(
            src_ref=group_send.at[peers[i]],
            dst_ref=group_recv.at[i],
            send_sem=group_send_sem.at[i],
            recv_sem=group_recv_sem.at[i],
            device_id={"chord": peers[i]},
            device_id_type=MESH,
        )
        copy.start()
        exchange.append(copy)

    def drain_span(side):
        for k in range(SWEEPS):
            for c in range(3):
                span_transfer(k, c, side).wait_send()

    def drain_rest(move, side):
        for k in range(SWEEPS):
            move(k, side).wait_send()

    on_span(drain_span)
    on_rest(drain_rest)

    total = group_send[me[2]]
    for i, copy in enumerate(exchange):
        copy.wait()
        total = total + group_recv[i + 1]
    patch_out[...] = total


def body(sizes, start, source, classes, table, cell, owner, normal, mode):
    _, cx, cy, cz = start.shape
    rows = cell.shape[0]
    chord_count = sizes[2]
    main = pl.BlockSpec(memory_space=pltpu.HBM)
    vmem = pltpu.VMEM
    dma = pltpu.SemaphoreType.DMA
    return pl.pallas_call(
        functools.partial(kernel, sizes),
        out_shape=(vmem(start.shape, F32), vmem((MODES, PATCH_DEV), F32)),
        in_specs=[main, main, main, pl.BlockSpec(memory_space=pltpu.SMEM), main, main, main, main],
        out_specs=(pl.BlockSpec(memory_space=vmem), pl.BlockSpec(memory_space=vmem)),
        scratch_shapes=[
            vmem(start.shape, F32),
            vmem(start.shape, F32),
            vmem((cx, cy, cz), jnp.int32),
            vmem((1, rows), jnp.int32),
            vmem((1, rows), jnp.int32),
            vmem((3, rows), F32),
            vmem((MODES, rows), F32),
            vmem((cx, cy, cz), F32),
            vmem((cx, cy, cz), F32),
            vmem((SWEEPS + 1, 3, cx, cy, cz), F32),
            vmem((SWEEPS, 2, 3, cy, cz), F32),
            vmem((SWEEPS, 2, 3, cx, cz), F32),
            vmem((SWEEPS, 2, 3, 8, cz), F32),
            vmem((SWEEPS, 2, 3, cx, cz), F32),
            vmem((SWEEPS, 3, 8, cz), F32),
            vmem((3, 1, rows), F32),
            vmem((3, cx * cy, 2 * cz), BF16),
            vmem((2 * cz, rows), BF16),
            vmem((chord_count * PATCH_DEV, rows), BF16),
            vmem((chord_count, MODES, PATCH_DEV), F32),
            vmem((chord_count, MODES, PATCH_DEV), F32),
            dma((7,)),
            dma((4,)),
            dma((SWEEPS, 5, 2)),
            dma((SWEEPS, 5, 2)),
            dma((chord_count,)),
            dma((chord_count,)),
        ],
        compiler_params=pltpu.CompilerParams(
            collective_id=0, has_side_effects=True, vmem_limit_bytes=63 * 1024 * 1024
        ),
        cost_estimate=pl.CostEstimate(
            flops=2 * 1024 * 1024 * 1024, bytes_accessed=3 * 1024 * 1024, transcendentals=0
        ),
    )(
        start,
        source,
        classes,
        table,
        cell.reshape(1, rows),
        owner.reshape(1, rows),
        normal,
        mode,
    )

def solution(mesh):
    sizes = tuple(mesh.shape[name] for name in AXES)
    field = P(None, "span", "pitch", "chord")
    listing = P(None, AXES)
    in_specs = (field, field, P(*AXES), P(), P(AXES), P(AXES, None), listing, listing)
    return jax.shard_map(
        functools.partial(body, sizes),
        mesh=mesh,
        in_specs=in_specs,
        out_specs=(field, listing),
        check_vma=False,
    )
```
